32 devices in a mesh: head: 2 (over x), seq: 16 (over z, y, core).
Axes of the slice: x: 2, y: 2, z: 4, core: 2. Of those that a mesh axis runs over, the one named last changes fastest.
Arguments:
- queries: bfloat16 [2, 1024, 4096], P(None, 'seq', 'head'), may hold values from -256 to 256
- keys: bfloat16 [2, 1024, 4096], P(None, 'seq', 'head'), may hold values from -256 to 256
- values: bfloat16 [2, 1024, 4096], P(None, 'seq', 'head'), may hold values from -6 to 6
- token_rates: float32 [1, 16, 1024], P(None, 'head', 'seq'), may hold values from 0.1 to 1
- step_size: float32 [16], P('head'), may hold values from 0.3 to 1
- w_gate: bfloat16 [16, 256, 512], P('head', 'seq'), may hold values from -0.375 to 0.375
- w_up: bfloat16 [16, 256, 512], P('head', 'seq'), may hold values from -0.375 to 0.375
- w_down: bfloat16 [16, 512, 256], P('head', 'seq'), may hold values from -0.25 to 0.25
- norm_gain: float32 [4096], replicated, may hold values from 0.5 to 1.5
Outputs:
- mixed: bfloat16 [2, 1024, 4096], P(None, ('seq', 'head'))
The draws below stay inside these ranges and needn't reach their ends.
All inputs are finite; a program needn't handle non-finite values.
Results may differ from the reference program's by a relative error of at most 0.0095.
Values may be sent and summed in bfloat16 or wider, within the bound.
A program may use at most 128 MiB of HBM per device.

```python
import math
import jax
import jax.numpy as jnp
from jax import lax

HEADS = 16
DH = 256
DF = 512
D = 4096
BLOCK = 1024
BLOCKS = 2
WIN = 512
NS_STEPS = 5


def pair_draw(key):
    base = jax.random.fold_in(key, 4242)
    key_query, key_key = jax.random.split(base, 2)
    shape = (BLOCKS, BLOCK, HEADS, DH)
    queries = 1.3 * jax.random.normal(key_query, shape, jnp.float32)
    keys = 1.3 * jax.random.normal(key_key, shape, jnp.float32)
    flat = (BLOCKS, BLOCK, HEADS * DH)
    return (jnp.clip(queries, -256.0, 256.0).reshape(flat), jnp.clip(keys, -256.0, 256.0).reshape(flat))


def draw_queries(key, part):
    return pair_draw(key)[0].astype(jnp.bfloat16)


def draw_keys(key, part):
    return pair_draw(key)[1].astype(jnp.bfloat16)


def shard_levels(own_key, dims, cuts, low, high):
    def one(dim, parts):
        draws = jax.random.uniform(jax.random.fold_in(jax.random.fold_in(own_key, 6), dim), (parts,), jnp.float32, low / len(cuts), high / len(cuts))
        return jnp.repeat(jnp.exp(draws), dims[dim] // parts).reshape((-1,) + (1,) * (len(dims) - dim - 1))

    loudness = one(*cuts[0])
    for cut in cuts[1:]:
        loudness = loudness * one(*cut)
    return loudness


def gaussian(stream_key, shape, spread, limit, pieces=(), kind=jnp.bfloat16):
    factor_of = shard_levels(stream_key, shape, pieces, -0.22, 0.18) if pieces else 1.0
    result = jax.random.normal(stream_key, shape, jnp.float32) * spread * factor_of
    return jnp.minimum(jnp.maximum(result, -limit), limit).astype(kind)


def setup_inputs(seed: int = 0) -> dict:
    streams_of = jax.random.split(jax.random.key(seed), 10)
    queries = draw_queries(jax.random.fold_in(streams_of[9], 71), 0)
    keys = draw_keys(jax.random.fold_in(streams_of[9], 71), 0)
    values = gaussian(streams_of[2], (BLOCKS, BLOCK, D), 1.0, 6.0, ((1, 16), (2, 2)))
    token_rates = jnp.clip(jnp.exp(math.log(1.0) - 2.3025851 * jax.random.uniform(streams_of[3], (BLOCKS - 1, HEADS, BLOCK), jnp.float32) ** shard_levels(streams_of[3], (BLOCKS - 1, HEADS, BLOCK), ((1, 2), (2, 16)), -0.2, 0.2)), 0.1, 1.0)
    step_size = jnp.clip(jnp.exp(math.log(1.0) - 1.2039728 * jax.random.uniform(streams_of[4], (HEADS,), jnp.float32) ** shard_levels(streams_of[4], (HEADS,), ((0, 2),), -0.2, 0.2)), 0.3, 1.0)
    w_gate = gaussian(streams_of[5], (HEADS, DH, DF), DH ** -0.5, 0.375, ((0, 2), (1, 16)))
    w_up = gaussian(streams_of[6], (HEADS, DH, DF), DH ** -0.5, 0.375, ((0, 2), (1, 16)))
    w_down = gaussian(streams_of[7], (HEADS, DF, DH), DF ** -0.5, 0.25, ((0, 2), (1, 16)))
    norm_gain = jnp.clip(1.0 + 0.1 * jax.random.normal(streams_of[8], (D,), jnp.float32), 0.5, 1.5)
    return dict(queries=queries, keys=keys, values=values, token_rates=token_rates, step_size=step_size, w_gate=w_gate, w_up=w_up, w_down=w_down, norm_gain=norm_gain)


def rms_norm(values_in):
    wide = values_in.astype(jnp.float32)
    mean_square = lax.optimization_barrier(jnp.mean(wide * wide, axis=-1, keepdims=True))
    return (wide * lax.rsqrt(mean_square + 1e-06)).astype(jnp.bfloat16)

def newton(grad_in):
    norm_value = jnp.sqrt(jnp.sum(grad_in * grad_in))
    iterate = grad_in / (norm_value + 1e-07)
    for _ in range(NS_STEPS):
        gram = jnp.dot(iterate, iterate.T, precision=lax.Precision.HIGHEST, preferred_element_type=jnp.float32)
        poly = -4.775 * gram + 2.0315 * jnp.dot(gram, gram, precision=lax.Precision.HIGHEST, preferred_element_type=jnp.float32)
        iterate = 3.4445 * iterate + jnp.dot(poly, iterate, precision=lax.Precision.HIGHEST, preferred_element_type=jnp.float32)
    return iterate

def window_head(query_h, key_h, value_h):
    total_len = query_h.shape[0]
    tile = math.gcd(total_len, 512)
    padding = jnp.zeros((WIN, DH), key_h.dtype)
    key_pad = jnp.concatenate([padding, key_h], 0)
    value_pad = jnp.concatenate([padding, value_h], 0)
    scale = 1.0 / math.sqrt(DH)

    def one_tile(tile_index):
        start = (tile_index * tile).astype(jnp.int32)
        query_tile = lax.dynamic_slice_in_dim(query_h, start, tile, 0)
        key_tile = lax.dynamic_slice_in_dim(key_pad, start, tile + WIN, 0)
        value_tile = lax.dynamic_slice_in_dim(value_pad, start, tile + WIN, 0)
        scores = jnp.dot(query_tile, key_tile.T, preferred_element_type=jnp.float32) * scale
        query_pos = start + jnp.arange(tile, dtype=jnp.int32)
        key_pos = start - WIN + jnp.arange(tile + WIN, dtype=jnp.int32)
        row_gap = query_pos[:, None] - key_pos[None, :]
        allowed = (row_gap >= 0) & (row_gap < WIN) & (key_pos[None, :] >= 0)
        scores = jnp.where(allowed, scores, -1e+30)
        row_top = lax.optimization_barrier(jnp.max(scores, axis=-1, keepdims=True))
        exp_scores = jnp.exp(scores - row_top)
        attn_weights = (exp_scores / lax.optimization_barrier(jnp.sum(exp_scores, axis=-1, keepdims=True))).astype(jnp.bfloat16)
        return jnp.dot(attn_weights, value_tile, preferred_element_type=jnp.float32)
    tiles = lax.map(one_tile, jnp.arange(total_len // tile, dtype=jnp.int32))
    return tiles.reshape(total_len, DH)

def fast_head(query_h, key_h, value_h, rates_h, step_h, gate_fast, up_fast, down_fast):
    outputs = []
    for block_index in range(BLOCKS):
        query_norm = rms_norm(query_h[block_index])
        gate_query = jnp.dot(query_norm, gate_fast, preferred_element_type=jnp.float32)
        up_query = jnp.dot(query_norm, up_fast, preferred_element_type=jnp.float32)
        hidden = (jax.nn.silu(gate_query) * up_query).astype(jnp.bfloat16)
        outputs.append(jnp.dot(hidden, down_fast, preferred_element_type=jnp.float32))
        if block_index < BLOCKS - 1:
            keys_now = rms_norm(key_h[block_index])
            vals_now = value_h[block_index]
            gate_pre = jnp.dot(keys_now, gate_fast, preferred_element_type=jnp.float32)
            up_pre = jnp.dot(keys_now, up_fast, preferred_element_type=jnp.float32)
            back = jnp.dot(vals_now, down_fast.T, preferred_element_type=jnp.float32)
            rate_col = rates_h[block_index][:, None]
            sigmoid_val = jax.nn.sigmoid(gate_pre)
            act_val = gate_pre * sigmoid_val
            d_gate = (rate_col * back * up_pre * sigmoid_val * (1.0 + gate_pre * (1.0 - sigmoid_val))).astype(jnp.bfloat16)
            d_up = (rate_col * back * act_val).astype(jnp.bfloat16)
            h_rate = (rate_col * act_val * up_pre).astype(jnp.bfloat16)
            grad_gate = jnp.dot(keys_now.T, d_gate, preferred_element_type=jnp.float32)
            grad_up = jnp.dot(keys_now.T, d_up, preferred_element_type=jnp.float32)
            grad_down_t = jnp.dot(vals_now.T, h_rate, preferred_element_type=jnp.float32)
            gate_fast = (gate_fast.astype(jnp.float32) + step_h * newton(grad_gate)).astype(jnp.bfloat16)
            up_fast = (up_fast.astype(jnp.float32) + step_h * newton(grad_up)).astype(jnp.bfloat16)
            down_fast = (down_fast.astype(jnp.float32) + step_h * newton(grad_down_t).T).astype(jnp.bfloat16)
    return jnp.stack(outputs)

def reference(queries, keys, values, token_rates, step_size, w_gate, w_up, w_down, norm_gain):
    total_len = BLOCKS * BLOCK

    def per_head(head_index):
        column = (head_index * DH).astype(jnp.int32)
        query_h = lax.dynamic_slice_in_dim(queries, column, DH, 2)
        key_h = lax.dynamic_slice_in_dim(keys, column, DH, 2)
        value_h = lax.dynamic_slice_in_dim(values, column, DH, 2)
        attention = window_head(query_h.reshape(total_len, DH), key_h.reshape(total_len, DH), value_h.reshape(total_len, DH))
        attention = attention.reshape(BLOCKS, BLOCK, DH)
        fast_out = fast_head(query_h, key_h, value_h, token_rates[:, head_index], step_size[head_index], w_gate[head_index], w_up[head_index], w_down[head_index])
        return (fast_out + attention).astype(jnp.bfloat16)
    combined = lax.map(per_head, jnp.arange(HEADS, dtype=jnp.int32))
    combined = jnp.transpose(combined, (1, 2, 0, 3)).reshape(BLOCKS, BLOCK, D)
    wide = combined.astype(jnp.float32)
    mean_square = lax.optimization_barrier(jnp.mean(wide * wide, axis=-1, keepdims=True))
    return (wide * lax.rsqrt(mean_square + 1e-06) * norm_gain).astype(jnp.bfloat16)
```

```python
import functools
import math

import jax
import jax.numpy as jnp
from jax import lax
from jax.experimental import pallas as pl
from jax.experimental.pallas import tpu as pltpu
from jax.sharding import PartitionSpec as P

DH = 256
DF = 512
WIN = 512
NS_STEPS = 5
TILE = 256
F32 = jnp.float32
BF16 = jnp.bfloat16
NN = (((1,), (0,)), ((), ()))
NT = (((1,), (1,)), ((), ()))
TN = (((0,), (0,)), ((), ()))

K0, V0, WG, WU, WD, RATE, QQ0, QQ1, K1, V1 = range(10)
FIRST = (K0, V0, WG, WU, WD, RATE)
FIN = 10


def dot(a, b, dims=NN):
    return lax.dot_general(a, b, dims, preferred_element_type=F32)


def split(a):
    high = a.astype(BF16)
    return high, (a - high.astype(F32)).astype(BF16)


def dot3(a, b, dims=NN):
    return dot(a[0], b[0], dims) + (dot(a[0], b[1], dims) + dot(a[1], b[0], dims))


def rms(tile):
    wide = tile.astype(F32)
    mean_square = jnp.mean(wide * wide, axis=-1, keepdims=True)
    return (wide * lax.rsqrt(mean_square + 1e-06)).astype(BF16)


def kernel(cfg, *refs):
    heads_here, seq_count, head_devices, tok, length, gathered, out_type = cfg
    (q_in, k_in, v_in, rate_in, step_in, wg_in, wu_in, wd_in, gain_in, out_ref) = refs[:10]
    (kbuf, vbuf, qbuf, wg, wu, wd, rates, rate_col, grads, obuf, fin) = refs[10:21]
    send, recv, fwd_send, out_send = refs[21:]
    per_head = seq_count // heads_here
    x = lax.axis_index("head")
    s = lax.axis_index("seq")
    my_head = s // per_head
    member = s % per_head
    rows = tok // head_devices
    g_rows = DH // seq_count
    d_rows = DF // seq_count

    def at_rows(ref, start, size, step):
        return ref.at[pl.ds(pl.multiple_of(start, step), size)]

    def column(ref, block, h):
        return ref.at[block, :, pl.ds(pl.multiple_of(h * DH, DH), DH)]

    def routes(h, which):
        start = s * tok
        if which == K0:
            return column(k_in, 0, h), at_rows(kbuf, WIN + start, tok, tok), 1
        if which == V0:
            return column(v_in, 0, h), at_rows(vbuf, WIN + start, tok, tok), 1
        if which == WG:
            return wg_in.at[h], at_rows(wg, s * g_rows, g_rows, g_rows), 1
        if which == WU:
            return wu_in.at[h], at_rows(wu, s * g_rows, g_rows, g_rows), 1
        if which == WD:
            return wd_in.at[h], at_rows(wd, s * d_rows, d_rows, d_rows), 1
        if which == RATE:
            return rate_in.at[h], rates.at[s], 1
        if which == QQ0:
            return column(q_in, 0, h), at_rows(qbuf, start, tok, tok), 0
        if which == QQ1:
            return column(q_in, 1, h), at_rows(qbuf, start, tok, tok), 1
        if which == K1:
            return column(k_in, 1, h), at_rows(kbuf, WIN + length + start, tok, tok), 1
        return column(v_in, 1, h), at_rows(vbuf, WIN + length + start, tok, tok), 1

    def recv_of(which):
        return recv.at[QQ0 if which == QQ1 else which]

    def each(which_list, action):
        def one(j, carry):
            h = (my_head + j) % heads_here
            for which in which_list:
                if gathered and which in (WG, WU, WD):
                    continue
                src, dst, role = routes(h, which)
                dest = h * per_head + role
                remote = pltpu.make_async_remote_copy(
                    src, dst, send.at[which, h], recv_of(which),
                    device_id=(x, dest), device_id_type=pl.DeviceIdType.MESH,
                )
                if action == "start":

                    @pl.when(dest == s)
                    def _():
                        pltpu.make_async_copy(src, dst, recv_of(which)).start()

                    @pl.when(dest != s)
                    def _():
                        remote.start()
                else:

                    @pl.when(dest != s)
                    def _():
                        remote.wait_send()
            return carry

        lax.fori_loop(0, heads_here, one, 0)

    def arrived(ref, sem):
        pltpu.make_async_copy(ref, ref, sem).wait()

    first_block = pl.ds(WIN, length)
    second_block = pl.ds(WIN + length, length)
    owner = member < 2

    each(FIRST, "start")

    @pl.when(member == 0)
    def _():
        kbuf[pl.ds(0, WIN), :] = jnp.zeros((WIN, DH), BF16)
        vbuf[pl.ds(0, WIN), :] = jnp.zeros((WIN, DH), BF16)

    each(FIRST, "sent")
    each((K1, V1, QQ1, QQ0), "start")

    def forward():
        pairs = [
            (kbuf.at[first_block], K0), (vbuf.at[first_block], V0),
            (wg, WG), (wu, WU), (wd, WD),
        ]
        return [
            pltpu.make_async_remote_copy(
                ref, ref, fwd_send.at[which], recv.at[which],
                device_id=(x, my_head * per_head), device_id_type=pl.DeviceIdType.MESH,
            )
            for ref, which in pairs
        ]

    @pl.when(member == 1)
    def _():
        if gathered:
            for src, dst, which in ((wg_in, wg, WG), (wu_in, wu, WU), (wd_in, wd, WD)):
                pltpu.make_async_copy(src.at[my_head], dst, recv.at[which]).start()
        arrived(rates, recv.at[RATE])

        def spread(i, carry):
            row = rates[i][0:1, :]
            col = jnp.broadcast_to(row, (128, 128)).T
            rate_col[pl.ds(pl.multiple_of(i * tok, tok), tok), :] = col[:tok]
            return carry

        lax.fori_loop(0, seq_count, spread, 0)
        arrived(kbuf.at[first_block], recv.at[K0])
        arrived(vbuf.at[first_block], recv.at[V0])
        arrived(wg, recv.at[WG])
        arrived(wu, recv.at[WU])
        arrived(wd, recv.at[WD])
        for copy in forward():
            copy.start()

        grads[...] = jnp.zeros_like(grads)

        def grad_tile(i, carry):
            place = pl.ds(pl.multiple_of(WIN + i * TILE, TILE), TILE)
            kn = rms(kbuf[place, :])
            vals = vbuf[place, :]
            gate_pre = dot(kn, wg[...])
            up_pre = dot(kn, wu[...])
            back = dot(vals, wd[...], NT)
            rate = rate_col[pl.ds(pl.multiple_of(i * TILE, TILE), TILE), 0:1]
            sig = jax.nn.sigmoid(gate_pre)
            act = gate_pre * sig
            rate_back = rate * back
            d_gate = (rate_back * up_pre * sig * (1.0 + gate_pre * (1.0 - sig))).astype(BF16)
            d_up = (rate_back * act).astype(BF16)
            h_rate = (rate * act * up_pre).astype(BF16)
            grads[0] += dot(kn, d_gate, TN)
            grads[1] += dot(kn, d_up, TN)
            grads[2] += dot(vals, h_rate, TN)
            return carry

        lax.fori_loop(0, length // TILE, grad_tile, 0)

        for p in range(3):
            g = grads[p]
            total = jnp.sum(jnp.sum(g * g, axis=1, keepdims=True), axis=0, keepdims=True)
            grads[p] = g / (jnp.sqrt(total) + 1e-07)

        def newton(i, carry):
            its = [grads[p] for p in range(3)]
            parts = [split(it) for it in its]
            grams = [dot3(part, part, NT) for part in parts]
            gram_parts = [split(gram) for gram in grams]
            polys = [
                -4.775 * gram + 2.0315 * dot3(gp, gp)
                for gram, gp in zip(grams, gram_parts)
            ]
            for p in range(3):
                grads[p] = 3.4445 * its[p] + dot3(split(polys[p]), parts[p])
            return carry

        lax.fori_loop(0, NS_STEPS, newton, 0)
        for copy in forward():
            copy.wait_send()
        step = step_in[my_head]
        wg[...] = (wg[...].astype(F32) + step * grads[0]).astype(BF16)
        wu[...] = (wu[...].astype(F32) + step * grads[1]).astype(BF16)
        wd[...] = (wd[...].astype(F32) + step * grads[2].T).astype(BF16)
        arrived(kbuf.at[second_block], recv.at[K1])
        arrived(vbuf.at[second_block], recv.at[V1])

    @pl.when(member == 0)
    def _():
        arrived(kbuf.at[first_block], recv.at[K0])
        arrived(vbuf.at[first_block], recv.at[V0])
        arrived(wg, recv.at[WG])
        arrived(wu, recv.at[WU])
        arrived(wd, recv.at[WD])

    @pl.when(owner)
    def _():
        arrived(qbuf, recv.at[QQ0])
        head_column = pl.ds(pl.multiple_of((x * heads_here + my_head) * DH, DH), DH)
        per_tile = TILE // rows

        def tile_step(i, carry):
            place = pl.ds(pl.multiple_of(i * TILE, TILE), TILE)
            q = qbuf[place, :]
            base = member * length + i * TILE
            span = pl.ds(pl.multiple_of(base, TILE), TILE + WIN)
            scores = dot(q, kbuf[span, :], NT) * (1.0 / math.sqrt(DH))
            r = lax.broadcasted_iota(jnp.int32, scores.shape, 0)
            c = lax.broadcasted_iota(jnp.int32, scores.shape, 1)
            gap = r + WIN - c
            allowed = (gap >= 0) & (gap < WIN) & (c + (base - WIN) >= 0)
            scores = jnp.where(allowed, scores, -1e30)
            e = jnp.exp(scores - jnp.max(scores, axis=-1, keepdims=True))
            probs = (e / jnp.sum(e, axis=-1, keepdims=True)).astype(BF16)
            attn = dot(probs, vbuf[span, :])
            qn = rms(q)
            gate = dot(qn, wg[...])
            up = dot(qn, wu[...])
            hidden = (gate * jax.nn.sigmoid(gate) * up).astype(BF16)
            fast = dot(hidden, wd[...])
            obuf[place, :] = (fast + attn).astype(BF16).astype(out_type)

            def ship(j, inner):
                number = i * per_tile + j
                ds, dx = number // head_devices, number % head_devices
                src = obuf.at[pl.ds(pl.multiple_of(number * rows, rows), rows)]
                dst = fin.at[member, :, head_column]
                mine = (ds == s) & (dx == x)

                @pl.when(mine)
                def _():
                    pltpu.make_async_copy(src, dst, recv.at[FIN + member]).start()

                @pl.when(jnp.logical_not(mine))
                def _():
                    pltpu.make_async_remote_copy(
                        src, dst, out_send.at[0], recv.at[FIN + member],
                        device_id=(dx, ds), device_id_type=pl.DeviceIdType.MESH,
                    ).start()

                return inner

            lax.fori_loop(0, per_tile, ship, 0)
            return carry

        lax.fori_loop(0, length // TILE, tile_step, 0)

    each((K1, V1, QQ1, QQ0), "sent")
    for block in range(2):
        arrived(fin.at[block], recv.at[FIN + block])
        wide = fin[block].astype(F32)
        mean_square = jnp.mean(wide * wide, axis=-1, keepdims=True)
        out_ref[block] = (wide * lax.rsqrt(mean_square + 1e-06) * gain_in[...]).astype(BF16)

    @pl.when(owner)
    def _():
        left = obuf.at[pl.ds(0, length - rows)]
        pltpu.make_async_copy(left, left, out_send.at[0]).wait()


def body(queries, keys, values, token_rates, step_size, w_gate, w_up, w_down, norm_gain):
    blocks, tok, width = queries.shape
    heads_here = width // DH
    seq_count = lax.axis_size("seq")
    head_devices = lax.axis_size("head")
    length = tok * seq_count
    rows = tok // head_devices
    gathered = w_gate.shape[1] % 16 != 0
    if gathered:
        w_gate, w_up, w_down = (
            lax.all_gather(w, "seq", axis=1, tiled=True) for w in (w_gate, w_up, w_down)
        )
    out_type = BF16 if rows % 16 == 0 else F32
    rate = jnp.pad(token_rates[0], ((0, 0), (0, 128 - tok)))
    rate = jnp.broadcast_to(rate[:, None, :], (heads_here, 8, 128))
    cfg = (heads_here, seq_count, head_devices, tok, length, gathered, out_type)
    hbm = pl.BlockSpec(memory_space=pl.ANY)
    vmem = pl.BlockSpec(memory_space=pltpu.VMEM)
    smem = pl.BlockSpec(memory_space=pltpu.SMEM)
    return pl.pallas_call(
        functools.partial(kernel, cfg),
        out_shape=jax.ShapeDtypeStruct((blocks, rows, width * head_devices), BF16),
        in_specs=[hbm, hbm, hbm, hbm, smem, hbm, hbm, hbm, vmem],
        out_specs=vmem,
        scratch_shapes=[
            pltpu.VMEM((WIN + 2 * length, DH), BF16),
            pltpu.VMEM((WIN + 2 * length, DH), BF16),
            pltpu.VMEM((length, DH), BF16),
            pltpu.VMEM((DH, DF), BF16),
            pltpu.VMEM((DH, DF), BF16),
            pltpu.VMEM((DF, DH), BF16),
            pltpu.VMEM((seq_count, 8, 128), F32),
            pltpu.VMEM((length, 128), F32),
            pltpu.VMEM((3, DH, DF), F32),
            pltpu.VMEM((length, DH), out_type),
            pltpu.VMEM((2, rows, width * head_devices), out_type),
            pltpu.SemaphoreType.DMA((10, heads_here)),
            pltpu.SemaphoreType.DMA((12,)),
            pltpu.SemaphoreType.DMA((5,)),
            pltpu.SemaphoreType.DMA((1,)),
        ],
        compiler_params=pltpu.CompilerParams(
            has_side_effects=True, vmem_limit_bytes=44 * 1024 * 1024
        ),
    )(
        queries, keys, values, rate, step_size, w_gate, w_up, w_down,
        norm_gain.reshape(1, -1),
    )


def solution(mesh):
    placed = (
        P(None, "seq", "head"),
        P(None, "seq", "head"),
        P(None, "seq", "head"),
        P(None, "head", "seq"),
        P("head"),
        P("head", "seq", None),
        P("head", "seq", None),
        P("head", "seq", None),
        P(),
    )
    return jax.shard_map(
        body, mesh=mesh, in_specs=placed, out_specs=P(None, ("seq", "head"), None), check_vma=False
    )
```

```python
import functools
import math

import jax
import jax.numpy as jnp
from jax import lax
from jax.experimental import pallas as pl
from jax.experimental.pallas import tpu as pltpu
from jax.sharding import PartitionSpec as P

DH = 256
DF = 512
WIN = 512
NS_STEPS = 5
TILE = 256
F32 = jnp.float32
BF16 = jnp.bfloat16
NN = (((1,), (0,)), ((), ()))
NT = (((1,), (1,)), ((), ()))
TN = (((0,), (0,)), ((), ()))

K0, V0, WG, WU, WD, RATE, QQ0, QQ1, K1, V1 = range(10)
FIRST = (K0, V0, WG, WU, WD, RATE)
FIN = 10


def dot(a, b, dims=NN):
    return lax.dot_general(a, b, dims, preferred_element_type=F32)


def split(a):
    high = a.astype(BF16)
    return high, (a - high.astype(F32)).astype(BF16)


def dot3(a, b, dims=NN):
    return dot(a[0], b[0], dims) + (dot(a[0], b[1], dims) + dot(a[1], b[0], dims))


def rms(tile):
    wide = tile.astype(F32)
    mean_square = jnp.mean(wide * wide, axis=-1, keepdims=True)
    return (wide * lax.rsqrt(mean_square + 1e-06)).astype(BF16)


def partner(head, number, count):
    if count & (count - 1):
        return (head + number) % count
    other, bit = 0, 1
    while bit < count:
        other = other + bit * ((head // bit + number // bit) % 2)
        bit *= 2
    return other


def kernel(cfg, *refs):
    heads_here, seq_count, head_devices, tok, length, gathered, out_type = cfg
    (q_in, k_in, v_in, rate_in, step_in, wg_in, wu_in, wd_in, gain_in, out_ref) = refs[:10]
    (kbuf, vbuf, qbuf, wg, wu, wd, rates, rate_col, grads, obuf, fin) = refs[10:21]
    send, recv, fwd_send, out_send = refs[21:]
    per_head = seq_count // heads_here
    x = lax.axis_index("head")
    s = lax.axis_index("seq")
    my_head = s // per_head
    member = s % per_head
    rows = tok // head_devices
    g_rows = DH // seq_count
    d_rows = DF // seq_count

    total = seq_count * head_devices
    barrier = pltpu.get_barrier_semaphore()

    def greet(i, carry):
        other = (x * seq_count + s + 1 + i) % total
        pl.semaphore_signal(
            barrier, inc=1, device_id=(other // seq_count, other % seq_count),
            device_id_type=pl.DeviceIdType.MESH,
        )
        return carry

    lax.fori_loop(0, total - 1, greet, 0)
    pl.semaphore_wait(barrier, total - 1)

    def at_rows(ref, start, size, step):
        return ref.at[pl.ds(pl.multiple_of(start, step), size)]

    def column(ref, block, h):
        return ref.at[block, :, pl.ds(pl.multiple_of(h * DH, DH), DH)]

    def routes(h, which):
        start = s * tok
        if which == K0:
            return column(k_in, 0, h), at_rows(kbuf, WIN + start, tok, tok), 1
        if which == V0:
            return column(v_in, 0, h), at_rows(vbuf, WIN + start, tok, tok), 1
        if which == WG:
            return wg_in.at[h], at_rows(wg, s * g_rows, g_rows, g_rows), 1
        if which == WU:
            return wu_in.at[h], at_rows(wu, s * g_rows, g_rows, g_rows), 1
        if which == WD:
            return wd_in.at[h], at_rows(wd, s * d_rows, d_rows, d_rows), 1
        if which == RATE:
            return rate_in.at[h], rates.at[s], 1
        if which == QQ0:
            return column(q_in, 0, h), at_rows(qbuf, start, tok, tok), 0
        if which == QQ1:
            return column(q_in, 1, h), at_rows(qbuf, start, tok, tok), 1
        if which == K1:
            return column(k_in, 1, h), at_rows(kbuf, WIN + length + start, tok, tok), 1
        return column(v_in, 1, h), at_rows(vbuf, WIN + length + start, tok, tok), 1

    def recv_of(which):
        return recv.at[QQ0 if which == QQ1 else which]

    def each(which_list, action):
        def one(j, carry):
            h = partner(my_head, heads_here - 1 - j, heads_here)
            for which in which_list:
                if gathered and which in (WG, WU, WD):
                    continue
                src, dst, role = routes(h, which)
                dest = h * per_head + role
                remote = pltpu.make_async_remote_copy(
                    src, dst, send.at[which, h], recv_of(which),
                    device_id=(x, dest), device_id_type=pl.DeviceIdType.MESH,
                )
                if action == "start":

                    @pl.when(dest == s)
                    def _():
                        pltpu.make_async_copy(src, dst, recv_of(which)).start()

                    @pl.when(dest != s)
                    def _():
                        remote.start()
                else:

                    @pl.when(dest != s)
                    def _():
                        remote.wait_send()
            return carry

        lax.fori_loop(0, heads_here, one, 0)

    def arrived(ref, sem):
        pltpu.make_async_copy(ref, ref, sem).wait()

    first_block = pl.ds(WIN, length)
    second_block = pl.ds(WIN + length, length)
    owner = member < 2

    each(FIRST, "start")

    @pl.when(member == 0)
    def _():
        kbuf[pl.ds(0, WIN), :] = jnp.zeros((WIN, DH), BF16)
        vbuf[pl.ds(0, WIN), :] = jnp.zeros((WIN, DH), BF16)

    each((K1, V1, QQ1, QQ0), "start")

    def forward():
        pairs = [
            (kbuf.at[first_block], K0), (vbuf.at[first_block], V0),
            (wg, WG), (wu, WU), (wd, WD),
        ]
        return [
            pltpu.make_async_remote_copy(
                ref, ref, fwd_send.at[which], recv.at[which],
                device_id=(x, my_head * per_head), device_id_type=pl.DeviceIdType.MESH,
            )
            for ref, which in pairs
        ]

    @pl.when(member == 1)
    def _():
        if gathered:
            for src, dst, which in ((wg_in, wg, WG), (wu_in, wu, WU), (wd_in, wd, WD)):
                pltpu.make_async_copy(src.at[my_head], dst, recv.at[which]).start()
        arrived(rates, recv.at[RATE])

        def spread(i, carry):
            row = rates[i][0:1, :]
            col = jnp.broadcast_to(row, (128, 128)).T
            rate_col[pl.ds(pl.multiple_of(i * tok, tok), tok), :] = col[:tok]
            return carry

        lax.fori_loop(0, seq_count, spread, 0)
        arrived(kbuf.at[first_block], recv.at[K0])
        arrived(vbuf.at[first_block], recv.at[V0])
        arrived(wg, recv.at[WG])
        arrived(wu, recv.at[WU])
        arrived(wd, recv.at[WD])
        for copy in forward():
            copy.start()

        grads[...] = jnp.zeros_like(grads)

        def grad_tile(i, carry):
            place = pl.ds(pl.multiple_of(WIN + i * TILE, TILE), TILE)
            kn = rms(kbuf[place, :])
            vals = vbuf[place, :]
            gate_pre = dot(kn, wg[...])
            up_pre = dot(kn, wu[...])
            back = dot(vals, wd[...], NT)
            rate = rate_col[pl.ds(pl.multiple_of(i * TILE, TILE), TILE), 0:1]
            sig = jax.nn.sigmoid(gate_pre)
            act = gate_pre * sig
            rate_back = rate * back
            d_gate = (rate_back * up_pre * sig * (1.0 + gate_pre * (1.0 - sig))).astype(BF16)
            d_up = (rate_back * act).astype(BF16)
            h_rate = (rate * act * up_pre).astype(BF16)
            grads[0] += dot(kn, d_gate, TN)
            grads[1] += dot(kn, d_up, TN)
            grads[2] += dot(vals, h_rate, TN)
            return carry

        lax.fori_loop(0, length // TILE, grad_tile, 0)

        for p in range(3):
            g = grads[p]
            total = jnp.sum(jnp.sum(g * g, axis=1, keepdims=True), axis=0, keepdims=True)
            grads[p] = g / (jnp.sqrt(total) + 1e-07)

        def newton(i, carry):
            its = [grads[p] for p in range(3)]
            parts = [split(it) for it in its]
            grams = [dot3(part, part, NT) for part in parts]
            gram_parts = [split(gram) for gram in grams]
            polys = [
                -4.775 * gram + 2.0315 * dot3(gp, gp)
                for gram, gp in zip(grams, gram_parts)
            ]
            for p in range(3):
                grads[p] = 3.4445 * its[p] + dot3(split(polys[p]), parts[p])
            return carry

        lax.fori_loop(0, NS_STEPS, newton, 0)
        for copy in forward():
            copy.wait_send()
        step = step_in[my_head]
        wg[...] = (wg[...].astype(F32) + step * grads[0]).astype(BF16)
        wu[...] = (wu[...].astype(F32) + step * grads[1]).astype(BF16)
        wd[...] = (wd[...].astype(F32) + step * grads[2].T).astype(BF16)
        arrived(kbuf.at[second_block], recv.at[K1])
        arrived(vbuf.at[second_block], recv.at[V1])

    @pl.when(member == 0)
    def _():
        arrived(kbuf.at[first_block], recv.at[K0])
        arrived(vbuf.at[first_block], recv.at[V0])
        arrived(wg, recv.at[WG])
        arrived(wu, recv.at[WU])
        arrived(wd, recv.at[WD])

    @pl.when(owner)
    def _():
        arrived(qbuf, recv.at[QQ0])
        head_column = pl.ds(pl.multiple_of((x * heads_here + my_head) * DH, DH), DH)
        per_tile = TILE // rows

        def tile_step(i, carry):
            place = pl.ds(pl.multiple_of(i * TILE, TILE), TILE)
            q = qbuf[place, :]
            base = member * length + i * TILE
            span = pl.ds(pl.multiple_of(base, TILE), TILE + WIN)
            scores = dot(q, kbuf[span, :], NT) * (1.0 / math.sqrt(DH))
            r = lax.broadcasted_iota(jnp.int32, scores.shape, 0)
            c = lax.broadcasted_iota(jnp.int32, scores.shape, 1)
            gap = r + WIN - c
            allowed = (gap >= 0) & (gap < WIN) & (c + (base - WIN) >= 0)
            scores = jnp.where(allowed, scores, -1e30)
            e = jnp.exp(scores - jnp.max(scores, axis=-1, keepdims=True))
            probs = (e / jnp.sum(e, axis=-1, keepdims=True)).astype(BF16)
            attn = dot(probs, vbuf[span, :])
            qn = rms(q)
            gate = dot(qn, wg[...])
            up = dot(qn, wu[...])
            hidden = (gate * jax.nn.sigmoid(gate) * up).astype(BF16)
            fast = dot(hidden, wd[...])
            obuf[place, :] = (fast + attn).astype(BF16).astype(out_type)

            def ship(j, inner):
                number = i * per_tile + j
                ds, dx = number // head_devices, number % head_devices
                src = obuf.at[pl.ds(pl.multiple_of(number * rows, rows), rows)]
                dst = fin.at[member, :, head_column]
                mine = (ds == s) & (dx == x)

                @pl.when(mine)
                def _():
                    pltpu.make_async_copy(src, dst, recv.at[FIN + member]).start()

                @pl.when(jnp.logical_not(mine))
                def _():
                    pltpu.make_async_remote_copy(
                        src, dst, out_send.at[0], recv.at[FIN + member],
                        device_id=(dx, ds), device_id_type=pl.DeviceIdType.MESH,
                    ).start()

                return inner

            lax.fori_loop(0, per_tile, ship, 0)
            return carry

        lax.fori_loop(0, length // TILE, tile_step, 0)

    each((K1, V1, QQ1, QQ0) + FIRST, "sent")
    for block in range(2):
        arrived(fin.at[block], recv.at[FIN + block])
        wide = fin[block].astype(F32)
        mean_square = jnp.mean(wide * wide, axis=-1, keepdims=True)
        out_ref[block] = (wide * lax.rsqrt(mean_square + 1e-06) * gain_in[...]).astype(BF16)

    @pl.when(owner)
    def _():
        left = obuf.at[pl.ds(0, length - rows)]
        pltpu.make_async_copy(left, left, out_send.at[0]).wait()


def body(queries, keys, values, token_rates, step_size, w_gate, w_up, w_down, norm_gain):
    blocks, tok, width = queries.shape
    heads_here = width // DH
    seq_count = lax.axis_size("seq")
    head_devices = lax.axis_size("head")
    length = tok * seq_count
    rows = tok // head_devices
    gathered = w_gate.shape[1] % 16 != 0
    if gathered:
        w_gate, w_up, w_down = (
            lax.all_gather(w, "seq", axis=1, tiled=True) for w in (w_gate, w_up, w_down)
        )
    out_type = BF16 if rows % 16 == 0 else F32
    rate = jnp.pad(token_rates[0], ((0, 0), (0, 128 - tok)))
    rate = jnp.broadcast_to(rate[:, None, :], (heads_here, 8, 128))
    cfg = (heads_here, seq_count, head_devices, tok, length, gathered, out_type)
    hbm = pl.BlockSpec(memory_space=pltpu.HBM)
    vmem = pl.BlockSpec(memory_space=pltpu.VMEM)
    smem = pl.BlockSpec(memory_space=pltpu.SMEM)
    return pl.pallas_call(
        functools.partial(kernel, cfg),
        out_shape=jax.ShapeDtypeStruct((blocks, rows, width * head_devices), BF16),
        in_specs=[hbm, hbm, hbm, hbm, smem, hbm, hbm, hbm, vmem],
        out_specs=vmem,
        scratch_shapes=[
            pltpu.VMEM((WIN + 2 * length, DH), BF16),
            pltpu.VMEM((WIN + 2 * length, DH), BF16),
            pltpu.VMEM((length, DH), BF16),
            pltpu.VMEM((DH, DF), BF16),
            pltpu.VMEM((DH, DF), BF16),
            pltpu.VMEM((DF, DH), BF16),
            pltpu.VMEM((seq_count, 8, 128), F32),
            pltpu.VMEM((length, 128), F32),
            pltpu.VMEM((3, DH, DF), F32),
            pltpu.VMEM((length, DH), out_type),
            pltpu.VMEM((2, rows, width * head_devices), out_type),
            pltpu.SemaphoreType.DMA((10, heads_here)),
            pltpu.SemaphoreType.DMA((12,)),
            pltpu.SemaphoreType.DMA((5,)),
            pltpu.SemaphoreType.DMA((1,)),
        ],
        compiler_params=pltpu.CompilerParams(
            has_side_effects=True, collective_id=0, vmem_limit_bytes=63 * 1024 * 1024
        ),
    )(
        queries, keys, values, rate, step_size, w_gate, w_up, w_down,
        norm_gain.reshape(1, -1),
    )


def solution(mesh):
    placed = (
        P(None, "seq", "head"),
        P(None, "seq", "head"),
        P(None, "seq", "head"),
        P(None, "head", "seq"),
        P("head"),
        P("head", "seq", None),
        P("head", "seq", None),
        P("head", "seq", None),
        P(),
    )
    return jax.shard_map(
        body, mesh=mesh, in_specs=placed, out_specs=P(None, ("seq", "head"), None), check_vma=False
    )
```
